32 devices in a mesh: box: 8 (over z, core), dir: 4 (over y, x).
Axes of the slice: x: 2, y: 2, z: 4, core: 2. Of those that a mesh axis runs over, the one named last changes fastest.
Arguments:
- child_spectra: bfloat16 [256, 24, 48, 256], P(('box', 'dir')), may hold values from -6 to 6
- child_ids: int32 [256], P('box'), may hold values from 0 to 511, as said below
- translators: bfloat16 [2, 316, 48, 96], P(None, None, None, 'dir'), may hold values from -0.75 to 0.75
- trans_index: int32 [64, 64], replicated, may hold values from 0 to 316
Outputs:
- parent_spectra: bfloat16 [64, 48, 96, 256], P('box', None, 'dir')
- incoming: bfloat16 [64, 48, 96, 256], P('box', None, 'dir')
The draws below stay inside these ranges and needn't reach their ends.
Inputs may be any that keep to these rules, and one draw needn't show every extreme that they name: child_ids never fall; every parent index below 64 has 1 to 8 children with distinct octants, and each box row has a parent with all 8; the children on box row r (positions r * 32 to (r+1) * 32 - 1) belong to parents r * 8 to (r+1) * 8 - 1, except 1 to 3 last ones on every row but the last, which belong to parent (r+1) * 8. `trans_index`: 0 marks a pair without translation; k > 0 selects operator k - 1.
All inputs are finite; a program needn't handle non-finite values.
Results may differ from the reference program's by a relative error of at most 0.0069.
Values may be sent and summed in bfloat16 or wider, within the bound.
A program may use at most 128 MiB of HBM per device.

```python
import jax
import jax.numpy as jnp
import numpy as np
from jax import lax

THETA_C = 24
PHI_C = 48
RHS = 128
NTRANS = 316
CH_ROW = 32
THETA_P = 48
PHI_P = 96
PAR_ROW = 8
NCH = 256
NPAR = 64
N_BOX = 8


def draw_child_ids(key, part):
    row_count = NCH // CH_ROW
    key_cut, key_full, key_units, key_octants = jax.random.split(key, 4)
    straddle = jax.random.randint(key_cut, (row_count,), 1, 4)
    straddle = jnp.where(jnp.arange(row_count) < row_count - 1, straddle, 0)
    before = jnp.concatenate([jnp.zeros((1,), jnp.int32), straddle[:-1]])
    totals = CH_ROW + before - straddle
    full_slot = jax.random.randint(key_full, (row_count,), 1, PAR_ROW)
    slot_range = jnp.arange(PAR_ROW)
    base_count = jnp.where(slot_range[None, :] == 0, 4, 1)
    base_count = jnp.where(slot_range[None, :] == full_slot[:, None], 8, base_count)
    spare_room = 8 - base_count
    unit_slot = jnp.arange(PAR_ROW * 7) // 7
    unit_level = jnp.arange(PAR_ROW * 7) % 7
    usable = unit_level[None, :] < spare_room[:, unit_slot]
    scores = jax.vmap(lambda subkey: jax.random.permutation(subkey, PAR_ROW * 7))(jax.random.split(key_units, row_count))
    scores = jnp.where(usable, scores, scores + PAR_ROW * 7)
    rank_order = jnp.argsort(jnp.argsort(scores, axis=1), axis=1)
    needed = totals - jnp.sum(base_count, axis=1)
    chosen = (rank_order < needed[:, None]).astype(jnp.int32)
    counts = base_count + jnp.sum(chosen.reshape(row_count, PAR_ROW, 7), axis=2)
    counts = counts.reshape(-1)
    slot_ends = jnp.cumsum(counts)
    positions = jnp.arange(NCH)
    parent = jnp.sum((slot_ends[None, :] <= positions[:, None]).astype(jnp.int32), axis=1)
    starts = slot_ends - counts
    within = positions - starts[parent]
    octant_draws = jax.vmap(lambda subkey: jax.random.permutation(subkey, 8))(jax.random.split(key_octants, NPAR))
    parent_range = jnp.arange(NPAR)
    octant_range = jnp.arange(8)
    favour = (parent_range == 0)[:, None] & (octant_range == 0)[None, :] | (parent_range == NPAR - 1)[:, None] & (octant_range == 7)[None, :]
    priority = jnp.where(favour, -1, octant_draws)
    picked = jnp.argsort(jnp.argsort(priority, axis=1), axis=1) < counts[:, None]
    ordering = jnp.argsort(jnp.where(picked, octant_range[None, :], octant_range[None, :] + 8), axis=1)
    octant = ordering[parent, within]
    return (8 * parent + octant).astype(jnp.int32)


def with_ends(entries, own_key, smallest, largest):
    longest = entries.shape.index(max(entries.shape))
    spots = []
    for shift in (0, 1):
        where = [jax.random.randint(jax.random.fold_in(own_key, axis), (), 0, length) for axis, length in enumerate(entries.shape)]
        where[longest] = (where[longest] + shift) % entries.shape[longest]
        spots.append(tuple(where))
    return entries.at[spots[0]].set(smallest).at[spots[1]].set(largest)


def steps_of(stream_key, shape, cuts, least, high):
    def one(dim, blocks):
        heights = jax.random.uniform(jax.random.fold_in(jax.random.fold_in(stream_key, 6), dim), (blocks,), jnp.float32, least / len(cuts), high / len(cuts))
        return jnp.repeat(jnp.exp(heights), shape[dim] // blocks).reshape((-1,) + (1,) * (len(shape) - dim - 1))

    gain = one(*cuts[0])
    for cut in cuts[1:]:
        gain = gain * one(*cut)
    return gain


def gaussian(own_key, dims, spread, limit, cuts=(), kind=jnp.bfloat16):
    loudness = steps_of(own_key, dims, cuts, -0.22, 0.18) if cuts else 1.0
    result = jax.random.normal(own_key, dims, jnp.float32) * spread * loudness
    return jnp.minimum(jnp.maximum(result, -limit), limit).astype(kind)


def setup_inputs(seed: int = 0) -> dict:
    key_of = jax.random.split(jax.random.key(seed), 5)
    return {
        "child_spectra": gaussian(key_of[0], (NCH, THETA_C, PHI_C, 2 * RHS), 1.0, 6.0, ((0, 32),)),
        "child_ids": draw_child_ids(jax.random.fold_in(key_of[4], 71), 0),
        "translators": gaussian(key_of[2], (2, NTRANS, THETA_P, PHI_P), NPAR ** -0.5, 0.75, ((3, 4),)),
        "trans_index": with_ends(jax.random.randint(key_of[3], (NPAR, NPAR), 0, NTRANS + 1), jax.random.fold_in(key_of[3], 1), 0, NTRANS).astype(jnp.int32),
    }


wave_shift = 5.0
midpoint_taps = (3.0, -25.0, 150.0, 150.0, -25.0, 3.0)


def theta_table(coarse_count):
    fine_count = 2 * coarse_count
    table_rows = np.zeros((fine_count, coarse_count))
    for target in range(fine_count):
        position = target / 2.0 - 0.25
        window_start = min(max(int(np.floor(position)) - 2, 0), coarse_count - 6)
        for tap_index in range(6):
            weight_value = 1.0
            for other_tap in range(6):
                if other_tap != tap_index:
                    weight_value *= (position - window_start - other_tap) / (tap_index - other_tap)
            table_rows[target, window_start + tap_index] = weight_value
    return table_rows


def phi_table(coarse_count):
    fine_count = 2 * coarse_count
    table_rows = np.zeros((fine_count, coarse_count))
    for target in range(fine_count):
        if target % 2 == 0:
            table_rows[target, target // 2] = 1.0
        else:
            middle = (target - 1) // 2
            for offset in range(6):
                table_rows[target, (middle - 2 + offset) % coarse_count] += midpoint_taps[offset] / 256.0
    return table_rows


def phase_factors(octants, theta_count, phi_angles):
    theta_angles = jnp.pi * (jnp.arange(theta_count, dtype=jnp.float32) + 0.5) / theta_count
    sign_x = ((octants % 2).astype(jnp.float32) * 2.0 - 1.0)[:, None, None]
    sign_y = (((octants // 2) % 2).astype(jnp.float32) * 2.0 - 1.0)[:, None, None]
    sign_z = ((octants // 4).astype(jnp.float32) * 2.0 - 1.0)[:, None, None]
    sine_theta = jnp.sin(theta_angles)[None, :, None]
    cosine_theta = jnp.cos(theta_angles)[None, :, None]
    angle_sum = wave_shift * (sign_x * sine_theta * jnp.cos(phi_angles)[None, None, :]
                              + sign_y * sine_theta * jnp.sin(phi_angles)[None, None, :]
                              + sign_z * cosine_theta)
    return jnp.cos(angle_sum), jnp.sin(angle_sum)


def rotate(lifted, cosine, sine):
    half = lifted.shape[-1] // 2
    real_part = lifted[..., :half]
    imag_part = lifted[..., half:]
    cosine = cosine[..., None]
    sine = sine[..., None]
    return jnp.concatenate([cosine * real_part - sine * imag_part, sine * real_part + cosine * imag_part], axis=-1)


def combine_terms(direct, cross):
    half = direct.shape[-1] // 2
    return jnp.concatenate([direct[..., :half] - cross[..., half:], direct[..., half:] + cross[..., :half]], axis=-1)


def reference(child_spectra, child_ids, translators, trans_index):
    theta_fine = jnp.asarray(theta_table(THETA_C), jnp.float32).astype(jnp.bfloat16).astype(jnp.float32)
    phi_fine = jnp.asarray(phi_table(PHI_C), jnp.float32).astype(jnp.bfloat16).astype(jnp.float32)
    phi_angles = 2.0 * jnp.pi * jnp.arange(PHI_P, dtype=jnp.float32) / PHI_P
    spectra_rows = child_spectra.reshape(N_BOX, CH_ROW, THETA_C, PHI_C, 2 * RHS)
    id_rows = child_ids.reshape(N_BOX, CH_ROW)

    def advance(accumulated, block_inputs):
        spectra_block, id_block = block_inputs
        widened = jnp.einsum('ctjr,gj->ctgr', spectra_block.astype(jnp.float32), phi_fine).astype(jnp.bfloat16)
        lifted = jnp.einsum('ctgr,ht->chgr', widened.astype(jnp.float32), theta_fine)
        cosine, sine = phase_factors(id_block % 8, THETA_P, phi_angles)
        shifted = rotate(lifted, cosine, sine).astype(jnp.bfloat16)
        accumulated = accumulated.at[(id_block // 8).astype(jnp.int32)].add(shifted.astype(jnp.float32))
        return accumulated, None

    start_sums = jnp.zeros((NPAR, THETA_P, PHI_P, 2 * RHS), jnp.float32)
    summed, unused = lax.scan(advance, start_sums, (spectra_rows, id_rows))
    parent_spectra = summed.astype(jnp.bfloat16)
    padded_ops = jnp.concatenate([jnp.zeros((2, 1, THETA_P, PHI_P), jnp.bfloat16), translators], axis=1)
    sources = parent_spectra.astype(jnp.float32)

    def per_theta(theta_row):
        operator_row = lax.dynamic_index_in_dim(padded_ops, theta_row, 2, keepdims=False)
        operators = jnp.take(operator_row, trans_index, axis=1).astype(jnp.float32)
        source_row = lax.dynamic_index_in_dim(sources, theta_row, 1, keepdims=False)
        direct = jnp.einsum('pqf,qfr->pfr', operators[0], source_row)
        cross = jnp.einsum('pqf,qfr->pfr', operators[1], source_row)
        return combine_terms(direct, cross)

    translated = lax.map(per_theta, jnp.arange(THETA_P, dtype=jnp.int32))
    incoming = jnp.transpose(translated, (1, 0, 2, 3)).astype(jnp.bfloat16)
    return parent_spectra, incoming
```

```python
import functools

import jax
import jax.numpy as jnp
import ml_dtypes
import numpy as np
from jax import lax
from jax.experimental import pallas as pl
from jax.experimental.pallas import tpu as pltpu
from jax.sharding import PartitionSpec as P

wave_shift = 5.0
midpoint_taps = (3.0, -25.0, 150.0, 150.0, -25.0, 3.0)
halo = 3
straddle = 3


def theta_table(coarse_count):
    fine_count = 2 * coarse_count
    table_rows = np.zeros((fine_count, coarse_count))
    for target in range(fine_count):
        position = target / 2.0 - 0.25
        window_start = min(max(int(np.floor(position)) - 2, 0), coarse_count - 6)
        for tap_index in range(6):
            weight_value = 1.0
            for other_tap in range(6):
                if other_tap != tap_index:
                    weight_value *= (position - window_start - other_tap) / (tap_index - other_tap)
            table_rows[target, window_start + tap_index] = weight_value
    return table_rows


def local_phi_table(local_count):
    table_rows = np.zeros((2 * local_count, local_count + 2 * halo))
    for target in range(2 * local_count):
        if target % 2 == 0:
            table_rows[target, target // 2 + halo] = 1.0
        else:
            middle = (target - 1) // 2
            for offset in range(6):
                table_rows[target, middle + 1 + offset] = midpoint_taps[offset] / 256.0
    return table_rows


def phase_factors(octants, theta_count, phi_angles):
    theta_angles = jnp.pi * (jnp.arange(theta_count, dtype=jnp.float32) + 0.5) / theta_count
    sign_x = ((octants % 2).astype(jnp.float32) * 2.0 - 1.0)[:, None, None]
    sign_y = ((octants // 2 % 2).astype(jnp.float32) * 2.0 - 1.0)[:, None, None]
    sign_z = ((octants // 4).astype(jnp.float32) * 2.0 - 1.0)[:, None, None]
    sine_theta = jnp.sin(theta_angles)[None, :, None]
    cosine_theta = jnp.cos(theta_angles)[None, :, None]
    angle_sum = wave_shift * (
        sign_x * sine_theta * jnp.cos(phi_angles)[None, None, :]
        + sign_y * sine_theta * jnp.sin(phi_angles)[None, None, :]
        + sign_z * cosine_theta
    )
    return (jnp.cos(angle_sum), jnp.sin(angle_sum))


def lift_kernel(pieces, group, parents, targets, slots, octants, *refs):
    blocks = refs[:pieces]
    ghosts = refs[pieces : 2 * pieces]
    weights = refs[2 * pieces : 3 * pieces]
    cosine, sine, out, send, total = refs[3 * pieces :]
    half = out.shape[-1] // 2
    step = pl.program_id(0)

    def add_child(position, sources, index):
        slot = slots[position]

        @pl.when((slot >= 0) & (slot < parents))
        def _():
            lifted = None
            for source, weight in zip(sources, weights):
                part = jnp.dot(weight[...], source[index], preferred_element_type=jnp.float32)
                lifted = part if lifted is None else lifted + part
            octant = octants[position]
            turn_cos = cosine[octant]
            turn_sin = sine[octant]
            real_part = lifted[:, :half]
            imag_part = lifted[:, half:]
            total[slot, :, :half] += turn_cos * real_part - turn_sin * imag_part
            total[slot, :, half:] += turn_sin * real_part + turn_cos * imag_part

    @pl.when(step == 0)
    def _():
        total[...] = jnp.zeros_like(total)

        @pl.loop(0, straddle)
        def _(index):
            add_child(index, ghosts, index)

    @pl.loop(0, group)
    def _(index):
        add_child(straddle + step * group + index, blocks, index)

    @pl.when(step == pl.num_programs(0) - 1)
    def _():
        rows = send.shape[2]
        for parent in range(parents):
            values = total[parent].astype(out.dtype)
            out[parent] = values
            for target in range(targets):
                send[target, parent] = values[target * rows : (target + 1) * rows]


def lift(pieces, ghosts, weights, cosine, sine, slots, octants, parents, targets):
    children = pieces[0].shape[0]
    group = 8
    rows = weights[0].shape[0]
    width = pieces[0].shape[-1]
    count = len(pieces)

    def whole(array):
        zeros = (0,) * array.ndim
        return pl.BlockSpec(array.shape, lambda step, *_: zeros)

    in_specs = [
        pl.BlockSpec((group,) + piece.shape[1:], lambda step, *_: (step, 0, 0)) for piece in pieces
    ]
    in_specs += [whole(array) for array in (*ghosts, *weights, cosine, sine)]
    out_shape = [
        jax.ShapeDtypeStruct((parents, rows, width), jnp.bfloat16),
        jax.ShapeDtypeStruct((targets, parents, rows // targets, width), jnp.bfloat16),
    ]
    flops = 2 * children * rows * width * sum(w.shape[1] for w in weights)
    return pl.pallas_call(
        functools.partial(lift_kernel, count, group, parents, targets),
        grid_spec=pltpu.PrefetchScalarGridSpec(
            num_scalar_prefetch=2,
            grid=(children // group,),
            in_specs=in_specs,
            out_specs=[whole(shape) for shape in out_shape],
            scratch_shapes=[pltpu.VMEM((parents, rows, width), jnp.float32)],
        ),
        out_shape=out_shape,
        compiler_params=pltpu.CompilerParams(vmem_limit_bytes=48 * 2**20),
        cost_estimate=pl.CostEstimate(
            flops=4 * flops, bytes_accessed=sum(p.size for p in pieces) * 2, transcendentals=0
        ),
        name="lift",
    )(slots, octants, *pieces, *ghosts, *weights, cosine, sine)


def translate_kernel(operators, sources, out):
    half = out.shape[-1] // 2
    for index in range(out.shape[0]):
        spectra = sources[index]
        direct = jnp.dot(operators[0, index], spectra, preferred_element_type=jnp.float32)
        cross = jnp.dot(operators[1, index], spectra, preferred_element_type=jnp.float32)
        out[index, :, :half] = (direct[:, :half] - cross[:, half:]).astype(out.dtype)
        out[index, :, half:] = (direct[:, half:] + cross[:, :half]).astype(out.dtype)


def translate(operators, sources):
    points, parents, width = sources.shape
    group = next(size for size in (8, 6, 4, 3, 2, 1) if points % size == 0)
    return pl.pallas_call(
        translate_kernel,
        grid=(points // group,),
        in_specs=[
            pl.BlockSpec((2, group, parents, parents), lambda step: (0, step, 0, 0)),
            pl.BlockSpec((group, parents, width), lambda step: (step, 0, 0)),
        ],
        out_specs=pl.BlockSpec((group, parents, width), lambda step: (step, 0, 0)),
        out_shape=jax.ShapeDtypeStruct(sources.shape, jnp.bfloat16),
        cost_estimate=pl.CostEstimate(
            flops=16 * points * parents * parents * width,
            bytes_accessed=8 * sources.size,
            transcendentals=0,
        ),
        name="translate",
    )(operators, sources)


def shared_out(block, ways):
    local_count = block.shape[2] // ways
    ring = jnp.concatenate([block[:, :, -halo:], block, block[:, :, :halo]], axis=2)
    width = local_count + 2 * halo
    parts = [ring[:, :, way * local_count : way * local_count + width] for way in range(ways)]
    stacked = jnp.stack(parts)
    return stacked.reshape(ways, block.shape[0], block.shape[1] * width, block.shape[3])


def chunk_plan(coarse_count, chunks):
    table = theta_table(coarse_count)
    fine_chunk = 2 * coarse_count // chunks
    needed = []
    for chunk in range(chunks):
        used = np.nonzero(table[chunk * fine_chunk : (chunk + 1) * fine_chunk].any(axis=0))[0]
        needed.append((int(used[0]), int(used[-1]) + 1))
    starts = [0] + [end for _, end in needed[:-1]]
    return [(start, end) for start, (_, end) in zip(starts, needed)], needed


def local(child_spectra, child_ids, translators, trans_index):
    ways = lax.axis_size("dir")
    rows = lax.axis_size("box")
    theta_coarse, phi_coarse, width = child_spectra.shape[1:]
    row_children = child_ids.shape[0]
    theta_fine = 2 * theta_coarse
    local_coarse = phi_coarse // ways
    local_fine = 2 * local_coarse
    parents_all = trans_index.shape[0]
    parents = parents_all // rows
    chunks = next(count for count in (3, 2, 1) if theta_fine % (count * rows) == 0)
    fine_chunk = theta_fine // chunks
    theta_local = fine_chunk // rows
    points = theta_local * local_fine
    box_rank = lax.axis_index("box")
    dir_rank = lax.axis_index("dir")
    segments, needed = chunk_plan(theta_coarse, chunks)

    forward = [(source, source + 1) for source in range(rows - 1)]
    ghost_ids = lax.ppermute(child_ids[-straddle:], "box", forward)
    ghost_ids = jnp.where(box_rank > 0, ghost_ids, -8)
    all_ids = jnp.concatenate([ghost_ids, child_ids])
    slots = all_ids // 8 - box_rank * parents
    octants = all_ids % 8

    columns, ghosts = [], []
    for start, end in segments:
        sent = shared_out(child_spectra[:, start:end], ways)
        got = lax.all_to_all(sent, "dir", split_axis=0, concat_axis=0, tiled=True)
        got = got.reshape((row_children,) + got.shape[2:])
        columns.append(got)
        ghosts.append(lax.ppermute(got[-straddle:], "box", forward))

    phi_index = (dir_rank * local_fine + jnp.arange(local_fine, dtype=jnp.int32)).astype(
        jnp.float32
    )
    phi_angles = 2.0 * jnp.pi * phi_index / (local_fine * ways)
    cosine, sine = phase_factors(jnp.arange(8, dtype=jnp.int32), theta_fine, phi_angles)

    def lanes(table, chunk):
        part = table[:, chunk * fine_chunk : (chunk + 1) * fine_chunk]
        part = part.reshape(8, fine_chunk * local_fine, 1)
        return jnp.broadcast_to(part, part.shape[:2] + (width // 2,))

    theta_weights = theta_table(theta_coarse).astype(ml_dtypes.bfloat16).astype(np.float64)
    phi_weights = local_phi_table(local_coarse)

    count = translators.shape[1]
    split = translators.reshape(2, count, chunks, rows, theta_local, local_fine)
    own = lax.dynamic_index_in_dim(split, box_rank, 3, keepdims=False)
    own = own.transpose(0, 2, 3, 4, 1).reshape(2 * chunks * points, count)
    chosen = trans_index.reshape(1, -1) - 1 == jnp.arange(count, dtype=jnp.int32)[:, None]
    operators = jnp.dot(own, chosen.astype(jnp.bfloat16), preferred_element_type=jnp.float32)
    operators = operators.astype(jnp.bfloat16)
    operators = operators.reshape(2, chunks, points, parents_all, parents_all)

    own_parts, sent_parts = [], []
    for chunk in range(chunks):
        low, high = needed[chunk]
        used = [
            index for index, (start, end) in enumerate(segments) if start < high and end > low
        ]
        weights = []
        for index in used:
            start, end = segments[index]
            table = np.einsum(
                "ht,gj->hgtj",
                theta_weights[chunk * fine_chunk : (chunk + 1) * fine_chunk, start:end],
                phi_weights,
            )
            table = table.reshape(fine_chunk * local_fine, -1)
            weights.append(jnp.asarray(table.astype(ml_dtypes.bfloat16)))
        part, sent = lift(
            [columns[index] for index in used],
            [ghosts[index] for index in used],
            weights,
            lanes(cosine, chunk),
            lanes(sine, chunk),
            slots,
            octants,
            parents,
            rows,
        )
        own_parts.append(part.reshape(parents, fine_chunk, local_fine, width))
        sent_parts.append(sent)

    results = []
    for chunk in range(chunks):
        got = lax.all_to_all(sent_parts[chunk], "box", split_axis=0, concat_axis=0, tiled=True)
        got = got.reshape(parents_all, points, width).transpose(1, 0, 2)
        moved = translate(operators[:, chunk], got).transpose(1, 0, 2)
        moved = moved.reshape(rows, parents, points, width)
        back = lax.all_to_all(moved, "box", split_axis=0, concat_axis=0, tiled=True)
        back = back.transpose(1, 0, 2, 3)
        results.append(back.reshape(parents, fine_chunk, local_fine, width))
    return jnp.concatenate(own_parts, axis=1), jnp.concatenate(results, axis=1)


def solution(mesh):
    return jax.shard_map(
        local,
        mesh=mesh,
        in_specs=(P(("box", "dir"), None, None, None), P("box"), P(None, None, None, "dir"), P()),
        out_specs=(P("box", None, "dir", None), P("box", None, "dir", None)),
        check_vma=False,
    )
```

```python
import functools

import jax
import jax.numpy as jnp
import ml_dtypes
import numpy as np
from jax import lax
from jax.experimental import pallas as pl
from jax.experimental.pallas import tpu as pltpu
from jax.sharding import PartitionSpec as P

wave_shift = 5.0
midpoint_taps = (3.0, -25.0, 150.0, 150.0, -25.0, 3.0)
halo = 3
straddle = 3


def theta_table(coarse_count):
    fine_count = 2 * coarse_count
    table_rows = np.zeros((fine_count, coarse_count))
    for target in range(fine_count):
        position = target / 2.0 - 0.25
        window_start = min(max(int(np.floor(position)) - 2, 0), coarse_count - 6)
        for tap_index in range(6):
            weight_value = 1.0
            for other_tap in range(6):
                if other_tap != tap_index:
                    weight_value *= (position - window_start - other_tap) / (tap_index - other_tap)
            table_rows[target, window_start + tap_index] = weight_value
    return table_rows


def local_phi_table(local_count):
    table_rows = np.zeros((2 * local_count, local_count + 2 * halo))
    for target in range(2 * local_count):
        if target % 2 == 0:
            table_rows[target, target // 2 + halo] = 1.0
        else:
            middle = (target - 1) // 2
            for offset in range(6):
                table_rows[target, middle + 1 + offset] = midpoint_taps[offset] / 256.0
    return table_rows


def phase_factors(octants, theta_count, phi_angles):
    theta_angles = jnp.pi * (jnp.arange(theta_count, dtype=jnp.float32) + 0.5) / theta_count
    sign_x = ((octants % 2).astype(jnp.float32) * 2.0 - 1.0)[:, None, None]
    sign_y = ((octants // 2 % 2).astype(jnp.float32) * 2.0 - 1.0)[:, None, None]
    sign_z = ((octants // 4).astype(jnp.float32) * 2.0 - 1.0)[:, None, None]
    sine_theta = jnp.sin(theta_angles)[None, :, None]
    cosine_theta = jnp.cos(theta_angles)[None, :, None]
    angle_sum = wave_shift * (
        sign_x * sine_theta * jnp.cos(phi_angles)[None, None, :]
        + sign_y * sine_theta * jnp.sin(phi_angles)[None, None, :]
        + sign_z * cosine_theta
    )
    return (jnp.cos(angle_sum), jnp.sin(angle_sum))


def lift_kernel(pieces, group, parents, slots, octants, *refs):
    blocks = refs[:pieces]
    ghosts = refs[pieces : 2 * pieces]
    weights = refs[2 * pieces : 3 * pieces]
    cosine, sine, out, send, total = refs[3 * pieces :]
    half = out.shape[-1] // 2
    step = pl.program_id(0)

    def add_child(position, sources, index):
        slot = slots[position]

        @pl.when((slot >= 0) & (slot < parents))
        def _():
            lifted = None
            for source, weight in zip(sources, weights):
                part = jnp.dot(weight[...], source[index], preferred_element_type=jnp.float32)
                lifted = part if lifted is None else lifted + part
            octant = octants[position]
            turn_cos = cosine[octant]
            turn_sin = sine[octant]
            real_part = lifted[:, :half]
            imag_part = lifted[:, half:]
            total[slot, :, :half] += turn_cos * real_part - turn_sin * imag_part
            total[slot, :, half:] += turn_sin * real_part + turn_cos * imag_part

    @pl.when(step == 0)
    def _():
        total[...] = jnp.zeros_like(total)

        @pl.loop(0, straddle)
        def _(index):
            add_child(index, ghosts, index)

    @pl.loop(0, group)
    def _(index):
        add_child(straddle + step * group + index, blocks, index)

    @pl.when(step == pl.num_programs(0) - 1)
    def _():
        out[...] = total[...].astype(out.dtype)
        tile = 8

        @pl.loop(0, total.shape[1] // tile)
        def _(index):
            block = total[:, pl.ds(pl.multiple_of(index * tile, tile), tile), :]
            block = jnp.swapaxes(block, 0, 1).reshape(tile * parents, block.shape[2])
            span = pl.ds(pl.multiple_of(index * tile * parents, tile * parents), tile * parents)
            send[span] = block.astype(send.dtype)


def lift(pieces, ghosts, weights, cosine, sine, slots, octants, parents):
    children = pieces[0].shape[0]
    group = 8
    rows = weights[0].shape[0]
    width = pieces[0].shape[-1]
    count = len(pieces)

    def whole(array):
        zeros = (0,) * array.ndim
        return pl.BlockSpec(array.shape, lambda step, *_: zeros)

    in_specs = [
        pl.BlockSpec((group,) + piece.shape[1:], lambda step, *_: (step, 0, 0)) for piece in pieces
    ]
    in_specs += [whole(array) for array in (*ghosts, *weights, cosine, sine)]
    out_shape = [
        jax.ShapeDtypeStruct((parents, rows, width), jnp.bfloat16),
        jax.ShapeDtypeStruct((rows * parents, width), jnp.bfloat16),
    ]
    flops = 2 * children * rows * width * sum(w.shape[1] for w in weights)
    return pl.pallas_call(
        functools.partial(lift_kernel, count, group, parents),
        grid_spec=pltpu.PrefetchScalarGridSpec(
            num_scalar_prefetch=2,
            grid=(children // group,),
            in_specs=in_specs,
            out_specs=[whole(shape) for shape in out_shape],
            scratch_shapes=[pltpu.VMEM((parents, rows, width), jnp.float32)],
        ),
        out_shape=out_shape,
        compiler_params=pltpu.CompilerParams(vmem_limit_bytes=48 * 2**20),
        cost_estimate=pl.CostEstimate(
            flops=4 * flops, bytes_accessed=sum(p.size for p in pieces) * 2, transcendentals=0
        ),
        name="lift",
    )(slots, octants, *pieces, *ghosts, *weights, cosine, sine)


def exchange_kernel(chunks, parents, ranks, *refs):
    sent = refs[:chunks]
    operators = refs[chunks : 2 * chunks]
    out, held, ready, send_sem, recv_sem, own_sem = refs[2 * chunks :]
    rows = held.shape[1] // chunks
    width = held.shape[2]
    half = width // 2
    me = lax.axis_index("box")

    barrier = pltpu.get_barrier_semaphore()
    for offset in range(1, ranks):
        pl.semaphore_signal(
            barrier,
            inc=1,
            device_id={"box": lax.rem(me + offset, ranks)},
            device_id_type=pl.DeviceIdType.MESH,
        )
    pl.semaphore_wait(barrier, ranks - 1)

    def remote(phase, chunk, offset):
        target = lax.rem(me + offset, ranks)
        span = pl.ds(chunk * rows, rows)
        source = sent[chunk].at[target] if phase == 0 else ready.at[target, span]
        landing = held if phase == 0 else out
        return pltpu.make_async_remote_copy(
            src_ref=source,
            dst_ref=landing.at[me, span],
            send_sem=send_sem.at[phase, chunk, offset - 1],
            recv_sem=recv_sem.at[phase, chunk, offset - 1],
            device_id={"box": target},
            device_id_type=pl.DeviceIdType.MESH,
        )

    def kept(phase, chunk):
        span = pl.ds(chunk * rows, rows)
        source = sent[chunk].at[me] if phase == 0 else ready.at[me, span]
        landing = held if phase == 0 else out
        return pltpu.make_async_copy(source, landing.at[me, span], own_sem.at[phase, chunk])

    order = sorted(range(1, ranks), key=lambda offset: abs(offset - ranks / 2))
    for chunk in range(chunks):
        for offset in order:
            remote(0, chunk, offset).start()
        kept(0, chunk).start()

    for chunk in range(chunks):
        for offset in order:
            remote(0, chunk, offset).wait_recv()
        kept(0, chunk).wait()
        table = operators[chunk]

        @pl.loop(0, rows // (2 * parents))
        def _(pair):
            span = pl.ds(pl.multiple_of(chunk * rows + pair * 2 * parents, 16), 2 * parents)
            both = [held[rank, span].astype(jnp.float32) for rank in range(ranks)]
            results = []
            for member in range(2):
                low = member * parents
                spectra = jnp.concatenate([value[low : low + parents] for value in both], axis=0)
                spectra = spectra.astype(jnp.bfloat16)
                product = jnp.dot(
                    table[2 * pair + member], spectra, preferred_element_type=jnp.float32
                )
                count = product.shape[0] // 2
                direct, cross = product[:count], product[count:]
                results.append(
                    jnp.concatenate(
                        [
                            direct[:, :half] - cross[:, half:],
                            direct[:, half:] + cross[:, :half],
                        ],
                        axis=1,
                    )
                )
            for rank in range(ranks):
                low = rank * parents
                value = jnp.concatenate(
                    [result[low : low + parents] for result in results], axis=0
                )
                ready[rank, span] = value.astype(jnp.bfloat16)

        for offset in order:
            remote(1, chunk, offset).start()
        kept(1, chunk).start()

    for chunk in range(chunks):
        for offset in order:
            remote(1, chunk, offset).wait_recv()
        kept(1, chunk).wait()
    for phase in range(2):
        for chunk in range(chunks):
            for offset in order:
                remote(phase, chunk, offset).wait_send()


def exchange(sent, operators, parents):
    chunks = len(sent)
    ranks, rows, width = sent[0].shape
    whole = (ranks, chunks * rows, width)
    in_specs = [pl.BlockSpec(memory_space=pl.ANY)] * chunks
    in_specs += [pl.BlockSpec(memory_space=pltpu.VMEM)] * chunks
    return pl.pallas_call(
        functools.partial(exchange_kernel, chunks, parents, ranks),
        in_specs=in_specs,
        out_specs=pl.BlockSpec(memory_space=pl.ANY),
        out_shape=jax.ShapeDtypeStruct(whole, jnp.bfloat16),
        scratch_shapes=[
            pltpu.VMEM(whole, jnp.bfloat16),
            pltpu.VMEM(whole, jnp.bfloat16),
            pltpu.SemaphoreType.DMA((2, chunks, ranks - 1)),
            pltpu.SemaphoreType.DMA((2, chunks, ranks - 1)),
            pltpu.SemaphoreType.DMA((2, chunks)),
        ],
        compiler_params=pltpu.CompilerParams(
            collective_id=0, has_side_effects=True, vmem_limit_bytes=40 * 2**20
        ),
        name="exchange",
    )(*sent, *operators)


def shared_out(block, ways):
    local_count = block.shape[2] // ways
    ring = jnp.concatenate([block[:, :, -halo:], block, block[:, :, :halo]], axis=2)
    width = local_count + 2 * halo
    parts = [ring[:, :, way * local_count : way * local_count + width] for way in range(ways)]
    stacked = jnp.stack(parts)
    return stacked.reshape(ways, block.shape[0], block.shape[1] * width, block.shape[3])


def chunk_plan(coarse_count, chunks):
    table = theta_table(coarse_count)
    fine_chunk = 2 * coarse_count // chunks
    needed = []
    for chunk in range(chunks):
        used = np.nonzero(table[chunk * fine_chunk : (chunk + 1) * fine_chunk].any(axis=0))[0]
        needed.append((int(used[0]), int(used[-1]) + 1))
    starts = [0] + [end for _, end in needed[:-1]]
    return [(start, end) for start, (_, end) in zip(starts, needed)], needed


def local(child_spectra, child_ids, translators, trans_index):
    ways = lax.axis_size("dir")
    rows = lax.axis_size("box")
    theta_coarse, phi_coarse, width = child_spectra.shape[1:]
    row_children = child_ids.shape[0]
    theta_fine = 2 * theta_coarse
    local_coarse = phi_coarse // ways
    local_fine = 2 * local_coarse
    parents_all = trans_index.shape[0]
    parents = parents_all // rows
    chunks = next(count for count in (3, 2, 1) if theta_fine % (count * rows) == 0)
    fine_chunk = theta_fine // chunks
    theta_local = fine_chunk // rows
    points = theta_local * local_fine
    box_rank = lax.axis_index("box")
    dir_rank = lax.axis_index("dir")
    segments, needed = chunk_plan(theta_coarse, chunks)

    forward = [(source, source + 1) for source in range(rows - 1)]
    ghost_ids = lax.ppermute(child_ids[-straddle:], "box", forward)
    ghost_ids = jnp.where(box_rank > 0, ghost_ids, -8)
    all_ids = jnp.concatenate([ghost_ids, child_ids])
    slots = all_ids // 8 - box_rank * parents
    octants = all_ids % 8

    columns, ghosts = [], []
    for start, end in segments:
        sent = shared_out(child_spectra[:, start:end], ways)
        got = lax.all_to_all(sent, "dir", split_axis=0, concat_axis=0, tiled=True)
        got = got.reshape((row_children,) + got.shape[2:])
        columns.append(got)
        ghosts.append(lax.ppermute(got[-straddle:], "box", forward))

    phi_index = (dir_rank * local_fine + jnp.arange(local_fine, dtype=jnp.int32)).astype(
        jnp.float32
    )
    phi_angles = 2.0 * jnp.pi * phi_index / (local_fine * ways)
    cosine, sine = phase_factors(jnp.arange(8, dtype=jnp.int32), theta_fine, phi_angles)

    def lanes(table, chunk):
        part = table[:, chunk * fine_chunk : (chunk + 1) * fine_chunk]
        part = part.reshape(8, fine_chunk * local_fine, 1)
        return jnp.broadcast_to(part, part.shape[:2] + (width // 2,))

    theta_weights = theta_table(theta_coarse).astype(ml_dtypes.bfloat16).astype(np.float64)
    phi_weights = local_phi_table(local_coarse)

    count = translators.shape[1]
    split = translators.reshape(2, count, chunks, rows, theta_local, local_fine)
    own = lax.dynamic_index_in_dim(split, box_rank, 3, keepdims=False)
    own = own.transpose(0, 2, 3, 4, 1).reshape(2 * chunks * points, count)
    chosen = trans_index.reshape(1, -1) - 1 == jnp.arange(count, dtype=jnp.int32)[:, None]
    operators = jnp.dot(own, chosen.astype(jnp.bfloat16), preferred_element_type=jnp.float32)
    operators = operators.astype(jnp.bfloat16)
    operators = operators.reshape(2, chunks, points, parents_all, parents_all)
    operators = operators.transpose(1, 2, 0, 3, 4)
    operators = operators.reshape(chunks, points, 2 * parents_all, parents_all)
    own_shape = (parents, theta_fine, local_fine, width)

    own_parts, sent_parts = [], []
    for chunk in range(chunks):
        low, high = needed[chunk]
        used = [
            index for index, (start, end) in enumerate(segments) if start < high and end > low
        ]
        weights = []
        for index in used:
            start, end = segments[index]
            table = np.einsum(
                "ht,gj->hgtj",
                theta_weights[chunk * fine_chunk : (chunk + 1) * fine_chunk, start:end],
                phi_weights,
            )
            table = table.reshape(fine_chunk * local_fine, -1)
            weights.append(jnp.asarray(table.astype(ml_dtypes.bfloat16)))
        part, sent = lift(
            [columns[index] for index in used],
            [ghosts[index] for index in used],
            weights,
            lanes(cosine, chunk),
            lanes(sine, chunk),
            slots,
            octants,
            parents,
        )
        own_parts.append(part.reshape(parents, fine_chunk, local_fine, width))
        sent_parts.append(sent.reshape(rows, points * parents, width))

    incoming = exchange(sent_parts, [operators[chunk] for chunk in range(chunks)], parents)
    incoming = incoming.reshape(rows, chunks, theta_local, local_fine, parents, width)
    incoming = incoming.transpose(4, 1, 0, 2, 3, 5).reshape(own_shape)
    return jnp.concatenate(own_parts, axis=1), incoming


def solution(mesh):
    return jax.shard_map(
        local,
        mesh=mesh,
        in_specs=(P(("box", "dir"), None, None, None), P("box"), P(None, None, None, "dir"), P()),
        out_specs=(P("box", None, "dir", None), P("box", None, "dir", None)),
        check_vma=False,
    )
```

```python
import functools

import jax
import jax.numpy as jnp
import ml_dtypes
import numpy as np
from jax import lax
from jax.experimental import pallas as pl
from jax.experimental.pallas import tpu as pltpu
from jax.sharding import PartitionSpec as P

wave_shift = 5.0
midpoint_taps = (3.0, -25.0, 150.0, 150.0, -25.0, 3.0)
halo = 3
straddle = 3


def theta_table(coarse_count):
    fine_count = 2 * coarse_count
    table_rows = np.zeros((fine_count, coarse_count))
    for target in range(fine_count):
        position = target / 2.0 - 0.25
        window_start = min(max(int(np.floor(position)) - 2, 0), coarse_count - 6)
        for tap_index in range(6):
            weight_value = 1.0
            for other_tap in range(6):
                if other_tap != tap_index:
                    weight_value *= (position - window_start - other_tap) / (tap_index - other_tap)
            table_rows[target, window_start + tap_index] = weight_value
    return table_rows


def local_phi_table(local_count):
    table_rows = np.zeros((2 * local_count, local_count + 2 * halo))
    for target in range(2 * local_count):
        if target % 2 == 0:
            table_rows[target, target // 2 + halo] = 1.0
        else:
            middle = (target - 1) // 2
            for offset in range(6):
                table_rows[target, middle + 1 + offset] = midpoint_taps[offset] / 256.0
    return table_rows


def phase_factors(octants, theta_count, phi_angles):
    theta_angles = jnp.pi * (jnp.arange(theta_count, dtype=jnp.float32) + 0.5) / theta_count
    sign_x = ((octants % 2).astype(jnp.float32) * 2.0 - 1.0)[:, None, None]
    sign_y = ((octants // 2 % 2).astype(jnp.float32) * 2.0 - 1.0)[:, None, None]
    sign_z = ((octants // 4).astype(jnp.float32) * 2.0 - 1.0)[:, None, None]
    sine_theta = jnp.sin(theta_angles)[None, :, None]
    cosine_theta = jnp.cos(theta_angles)[None, :, None]
    angle_sum = wave_shift * (
        sign_x * sine_theta * jnp.cos(phi_angles)[None, None, :]
        + sign_y * sine_theta * jnp.sin(phi_angles)[None, None, :]
        + sign_z * cosine_theta
    )
    return (jnp.cos(angle_sum), jnp.sin(angle_sum))


def spectra_kernel(chunks, parents, ranks, ways, plan, *refs):
    first, packed, refs = refs[0], refs[1:chunks], refs[chunks:]
    keeps, octants, signs, lasts, refs = *refs[:4], refs[4:]
    used = sum(len(pieces) for pieces in plan)
    flat_weights, refs = refs[:used], refs[used:]
    cosine, sine, refs = refs[:chunks], refs[chunks : 2 * chunks], refs[2 * chunks :]
    operators, refs = refs[:chunks], refs[chunks:]
    own_out, out, refs = refs[0], refs[1], refs[2:]
    columns, refs = refs[:chunks], refs[chunks:]
    running, staged, sent, held, ready = refs[:5]
    dir_send, dir_recv, ghost_send, ghost_recv, keep_sem, box_send, box_recv, own_sem = refs[5:]
    weights = []
    for pieces in plan:
        weights.append(flat_weights[: len(pieces)])
        flat_weights = flat_weights[len(pieces) :]

    rows = held.shape[1] // chunks
    points = running.shape[1]
    width = held.shape[2]
    half = width // 2
    children = columns[0].shape[0]
    share = (children - straddle) // ways
    me = lax.axis_index("box")
    side = lax.axis_index("dir")

    def to_box(target):
        return dict(device_id={"box": target}, device_id_type=pl.DeviceIdType.MESH)

    def to_dir(target):
        return dict(device_id={"dir": target}, device_id_type=pl.DeviceIdType.MESH)

    barrier = pltpu.get_barrier_semaphore()
    for offset in range(1, ranks):
        pl.semaphore_signal(barrier, inc=1, **to_box(lax.rem(me + offset, ranks)))
    for offset in range(1, ways):
        pl.semaphore_signal(barrier, inc=1, **to_dir(lax.rem(side + offset, ways)))
    pl.semaphore_wait(barrier, ranks + ways - 2)

    def dir_copy(piece, offset):
        target = lax.rem(side + offset, ways)
        return pltpu.make_async_remote_copy(
            src_ref=packed[piece - 1].at[target],
            dst_ref=columns[piece].at[pl.ds(straddle + side * share, share)],
            send_sem=dir_send.at[piece - 1, offset - 1],
            recv_sem=dir_recv.at[piece - 1, offset - 1],
            **to_dir(target),
        )

    def dir_kept(piece):
        if piece == 0:
            source, landing = first, columns[0].at[pl.ds(straddle, children - straddle)]
        else:
            source = packed[piece - 1].at[side]
            landing = columns[piece].at[pl.ds(straddle + side * share, share)]
        return pltpu.make_async_copy(source, landing, keep_sem.at[piece])

    def ghost_copy(piece):
        if piece == 0:
            source = first.at[pl.ds(children - 2 * straddle, straddle)]
        else:
            source = columns[piece].at[pl.ds(children - straddle, straddle)]
        return pltpu.make_async_remote_copy(
            src_ref=source,
            dst_ref=columns[piece].at[pl.ds(0, straddle)],
            send_sem=ghost_send.at[piece],
            recv_sem=ghost_recv.at[piece],
            **to_box(me + 1),
        )

    def box_copy(phase, chunk, offset):
        target = lax.rem(me + offset, ranks)
        span = pl.ds(chunk * rows, rows)
        if phase == 0:
            source = sent.at[chunk, pl.ds(pl.multiple_of(target * rows, 16), rows)]
        else:
            source = ready.at[target, span]
        landing = held if phase == 0 else out
        return pltpu.make_async_remote_copy(
            src_ref=source,
            dst_ref=landing.at[me, span],
            send_sem=box_send.at[phase, chunk, offset - 1],
            recv_sem=box_recv.at[phase, chunk, offset - 1],
            **to_box(target),
        )

    def box_kept(phase, chunk):
        span = pl.ds(chunk * rows, rows)
        if phase == 0:
            source = sent.at[chunk, pl.ds(pl.multiple_of(me * rows, 16), rows)]
        else:
            source = ready.at[me, span]
        landing = held if phase == 0 else out
        return pltpu.make_async_copy(source, landing.at[me, span], own_sem.at[phase, chunk])

    def own_copy(chunk):
        return pltpu.make_async_copy(
            staged.at[chunk], own_out.at[:, pl.ds(chunk * points, points)], own_sem.at[2, chunk]
        )

    order = sorted(range(1, ranks), key=lambda offset: abs(offset - ranks / 2))

    def forward_ghosts(piece):
        @pl.when(me < ranks - 1)
        def _():
            ghost_copy(piece).start()

    def await_ghosts(piece):
        @pl.when(me > 0)
        def _():
            ghost_copy(piece).wait_recv()

    forward_ghosts(0)
    dir_kept(0).start()
    for piece in range(1, chunks):
        for offset in range(1, ways):
            dir_copy(piece, offset).start()
        dir_kept(piece).start()

    @pl.when(me == 0)
    def _():
        for piece in range(chunks):
            columns[piece][0:straddle] = jnp.zeros((straddle,) + columns[piece].shape[1:], jnp.bfloat16)

    running[0] = jnp.zeros(running.shape[1:], jnp.float32)

    for chunk in range(chunks):
        dir_kept(chunk).wait()
        if chunk > 0:
            for offset in range(1, ways):
                dir_copy(chunk, offset).wait_recv()
            forward_ghosts(chunk)
        await_ghosts(chunk)

        @pl.loop(0, children)
        def _(child):
            lifted = None
            for piece, weight in zip(plan[chunk], weights[chunk]):
                part = jnp.dot(
                    weight[...], columns[piece][child], preferred_element_type=jnp.float32
                )
                lifted = part if lifted is None else lifted + part
            octant = octants[child]
            keep = keeps[child]
            turn_cos = cosine[chunk][octant]
            turn_sin = sine[chunk][octant] * signs[child]
            real_part = lifted[:, :half]
            imag_part = lifted[:, half:]
            running[child + 1, :, :half] = (
                keep * running[child, :, :half] + turn_cos * real_part - turn_sin * imag_part
            )
            running[child + 1, :, half:] = (
                keep * running[child, :, half:] + turn_sin * real_part + turn_cos * imag_part
            )

        @pl.loop(0, points // 16)
        def _(tile):
            span = pl.ds(pl.multiple_of(tile * 16, 16), 16)
            values = [running[lasts[parent], span, :] for parent in range(parents)]
            for parent in range(parents):
                staged[chunk, parent, span] = values[parent].astype(jnp.bfloat16)
            for part in range(2):
                block = jnp.stack([value[8 * part : 8 * part + 8] for value in values])
                block = jnp.swapaxes(block, 0, 1).reshape(8 * parents, width)
                low = pl.multiple_of((2 * tile + part) * 8 * parents, 8 * parents)
                sent[chunk, pl.ds(low, 8 * parents)] = block.astype(jnp.bfloat16)

        for offset in order:
            box_copy(0, chunk, offset).start()
        box_kept(0, chunk).start()
        own_copy(chunk).start()

    for chunk in range(chunks):
        for offset in order:
            box_copy(0, chunk, offset).wait_recv()
        box_kept(0, chunk).wait()
        table = operators[chunk]

        @pl.loop(0, rows // (2 * parents))
        def _(pair):
            span = pl.ds(pl.multiple_of(chunk * rows + pair * 2 * parents, 16), 2 * parents)
            both = [held[rank, span].astype(jnp.float32) for rank in range(ranks)]
            results = []
            for member in range(2):
                low = member * parents
                spectra = jnp.concatenate([value[low : low + parents] for value in both], axis=0)
                spectra = spectra.astype(jnp.bfloat16)
                product = jnp.dot(
                    table[2 * pair + member], spectra, preferred_element_type=jnp.float32
                )
                count = product.shape[0] // 2
                direct, cross = product[:count], product[count:]
                results.append(
                    jnp.concatenate(
                        [
                            direct[:, :half] - cross[:, half:],
                            direct[:, half:] + cross[:, :half],
                        ],
                        axis=1,
                    )
                )
            for rank in range(ranks):
                low = rank * parents
                value = jnp.concatenate(
                    [result[low : low + parents] for result in results], axis=0
                )
                ready[rank, span] = value.astype(jnp.bfloat16)

        for offset in order:
            box_copy(1, chunk, offset).start()
        box_kept(1, chunk).start()

    for chunk in range(chunks):
        for offset in order:
            box_copy(1, chunk, offset).wait_recv()
        box_kept(1, chunk).wait()
        own_copy(chunk).wait()

        @pl.when(me < ranks - 1)
        def _():
            ghost_copy(chunk).wait_send()

        if chunk > 0:
            for offset in range(1, ways):
                dir_copy(chunk, offset).wait_send()
        for phase in range(2):
            for offset in order:
                box_copy(phase, chunk, offset).wait_send()


def spectra(first, packed, scalars, plan, weights, cosine, sine, operators, parents, ranks):
    chunks = len(plan)
    ways = packed[0].shape[0]
    children = first.shape[0] + straddle
    width = first.shape[-1]
    points = weights[0][0].shape[0]
    rows = points * parents // ranks
    whole = (ranks, chunks * rows, width)
    arrays = [first, *packed, *scalars, *sum(weights, []), *cosine, *sine, *operators]
    in_specs = [pl.BlockSpec(memory_space=pl.ANY)] * chunks
    in_specs += [pl.BlockSpec(memory_space=pltpu.SMEM)] * len(scalars)
    in_specs += [pl.BlockSpec(memory_space=pltpu.VMEM)] * (len(arrays) - len(in_specs))
    piece_rows = [first.shape[1]] + [piece.shape[2] for piece in packed]
    dma = pltpu.SemaphoreType.DMA
    return pl.pallas_call(
        functools.partial(spectra_kernel, chunks, parents, ranks, ways, plan),
        in_specs=in_specs,
        out_specs=[pl.BlockSpec(memory_space=pl.ANY)] * 2,
        out_shape=[
            jax.ShapeDtypeStruct((parents, chunks * points, width), jnp.bfloat16),
            jax.ShapeDtypeStruct(whole, jnp.bfloat16),
        ],
        scratch_shapes=[
            *[pltpu.VMEM((children, count, width), jnp.bfloat16) for count in piece_rows],
            pltpu.VMEM((children + 1, points, width), jnp.float32),
            pltpu.VMEM((chunks, parents, points, width), jnp.bfloat16),
            pltpu.VMEM((chunks, ranks * rows, width), jnp.bfloat16),
            pltpu.VMEM(whole, jnp.bfloat16),
            pltpu.VMEM(whole, jnp.bfloat16),
            dma((chunks - 1, ways - 1)),
            dma((chunks - 1, ways - 1)),
            dma((chunks,)),
            dma((chunks,)),
            dma((chunks,)),
            dma((2, chunks, ranks - 1)),
            dma((2, chunks, ranks - 1)),
            dma((3, chunks)),
        ],
        compiler_params=pltpu.CompilerParams(
            collective_id=0, has_side_effects=True, vmem_limit_bytes=58 * 2**20
        ),
        name="spectra",
    )(*arrays)


def shared_out(block, ways):
    local_count = block.shape[2] // ways
    ring = jnp.concatenate([block[:, :, -halo:], block, block[:, :, :halo]], axis=2)
    width = local_count + 2 * halo
    parts = [ring[:, :, way * local_count : way * local_count + width] for way in range(ways)]
    stacked = jnp.stack(parts)
    stacked = stacked.reshape(ways, block.shape[0], block.shape[1] * width, block.shape[3])
    spare = -stacked.shape[2] % 16
    return jnp.pad(stacked, ((0, 0), (0, 0), (0, spare), (0, 0)))


def chunk_plan(coarse_count, chunks):
    table = theta_table(coarse_count)
    fine_chunk = 2 * coarse_count // chunks
    needed = []
    for chunk in range(chunks):
        used = np.nonzero(table[chunk * fine_chunk : (chunk + 1) * fine_chunk].any(axis=0))[0]
        needed.append((int(used[0]), int(used[-1]) + 1))
    starts = [0] + [end for _, end in needed[:-1]]
    return [(start, end) for start, (_, end) in zip(starts, needed)], needed


def local(child_spectra, child_ids, translators, trans_index):
    ways = lax.axis_size("dir")
    rows = lax.axis_size("box")
    theta_coarse, phi_coarse, width = child_spectra.shape[1:]
    row_children = child_ids.shape[0]
    theta_fine = 2 * theta_coarse
    local_coarse = phi_coarse // ways
    local_fine = 2 * local_coarse
    parents_all = trans_index.shape[0]
    parents = parents_all // rows
    chunks = next(count for count in (3, 2, 1) if theta_fine % (count * rows) == 0)
    fine_chunk = theta_fine // chunks
    theta_local = fine_chunk // rows
    points = theta_local * local_fine
    box_rank = lax.axis_index("box")
    dir_rank = lax.axis_index("dir")
    segments, needed = chunk_plan(theta_coarse, chunks)

    forward = [(source, source + 1) for source in range(rows - 1)]
    ghost_ids = lax.ppermute(child_ids[-straddle:], "box", forward)
    ghost_ids = jnp.where(box_rank > 0, ghost_ids, -8)
    all_ids = jnp.concatenate([ghost_ids, child_ids])
    slots = all_ids // 8 - box_rank * parents
    octants = all_ids % 8
    same = slots[1:] == slots[:-1]
    keeps = jnp.concatenate([jnp.zeros((1,), jnp.float32), same.astype(jnp.float32)])
    upper = octants >= 4
    signs = jnp.where(upper, 1.0, -1.0).astype(jnp.float32)
    mirrored = jnp.where(upper, octants - 4, 3 - octants)
    slot_range = jnp.arange(parents, dtype=jnp.int32)
    lasts = jnp.sum((slots[None, :] <= slot_range[:, None]).astype(jnp.int32), axis=1)

    packed = [shared_out(child_spectra[:, start:end], ways) for start, end in segments]
    first = lax.all_to_all(packed[0], "dir", split_axis=0, concat_axis=0, tiled=True)
    first = first.reshape((row_children,) + first.shape[2:])

    phi_index = (dir_rank * local_fine + jnp.arange(local_fine, dtype=jnp.int32)).astype(
        jnp.float32
    )
    phi_angles = 2.0 * jnp.pi * phi_index / (local_fine * ways)
    cosine, sine = phase_factors(jnp.arange(4, 8, dtype=jnp.int32), theta_fine, phi_angles)

    def lanes(table, chunk):
        part = table[:, chunk * fine_chunk : (chunk + 1) * fine_chunk]
        part = part.reshape(4, fine_chunk * local_fine, 1)
        return jnp.broadcast_to(part, part.shape[:2] + (width // 2,))

    theta_weights = theta_table(theta_coarse).astype(ml_dtypes.bfloat16).astype(np.float64)
    phi_weights = local_phi_table(local_coarse)

    count = translators.shape[1]
    split = translators.reshape(2, count, chunks, rows, theta_local, local_fine)
    own = lax.dynamic_index_in_dim(split, box_rank, 3, keepdims=False)
    own = own.transpose(0, 2, 3, 4, 1).reshape(2 * chunks * points, count)
    chosen = trans_index.reshape(1, -1) - 1 == jnp.arange(count, dtype=jnp.int32)[:, None]
    operators = jnp.dot(own, chosen.astype(jnp.bfloat16), preferred_element_type=jnp.float32)
    operators = operators.astype(jnp.bfloat16)
    operators = operators.reshape(2, chunks, points, parents_all, parents_all)
    operators = operators.transpose(1, 2, 0, 3, 4)
    operators = operators.reshape(chunks, points, 2 * parents_all, parents_all)
    own_shape = (parents, theta_fine, local_fine, width)

    plan, weights = [], []
    for chunk in range(chunks):
        low, high = needed[chunk]
        used = [
            index for index, (start, end) in enumerate(segments) if start < high and end > low
        ]
        tables = []
        for index in used:
            start, end = segments[index]
            table = np.einsum(
                "ht,gj->hgtj",
                theta_weights[chunk * fine_chunk : (chunk + 1) * fine_chunk, start:end],
                phi_weights,
            )
            table = table.reshape(fine_chunk * local_fine, -1)
            table = np.pad(table, ((0, 0), (0, -table.shape[1] % 16)))
            tables.append(jnp.asarray(table.astype(ml_dtypes.bfloat16)))
        plan.append(used)
        weights.append(tables)
    parent_spectra, incoming = spectra(
        first,
        packed[1:],
        (keeps, mirrored, signs, lasts),
        plan,
        weights,
        [lanes(cosine, chunk) for chunk in range(chunks)],
        [lanes(sine, chunk) for chunk in range(chunks)],
        [operators[chunk] for chunk in range(chunks)],
        parents,
        rows,
    )
    incoming = incoming.reshape(rows, chunks, theta_local, local_fine, parents, width)
    incoming = incoming.transpose(4, 1, 0, 2, 3, 5).reshape(own_shape)
    return parent_spectra.reshape(own_shape), incoming


def solution(mesh):
    return jax.shard_map(
        local,
        mesh=mesh,
        in_specs=(P(("box", "dir"), None, None, None), P("box"), P(None, None, None, "dir"), P()),
        out_specs=(P("box", None, "dir", None), P("box", None, "dir", None)),
        check_vma=False,
    )
```

```python
import functools

import jax
import jax.numpy as jnp
import ml_dtypes
import numpy as np
from jax import lax
from jax.experimental import pallas as pl
from jax.experimental.pallas import tpu as pltpu
from jax.sharding import PartitionSpec as P

wave_shift = 5.0
midpoint_taps = (3.0, -25.0, 150.0, 150.0, -25.0, 3.0)
halo = 3
straddle = 3


def theta_table(coarse_count):
    fine_count = 2 * coarse_count
    table_rows = np.zeros((fine_count, coarse_count))
    for target in range(fine_count):
        position = target / 2.0 - 0.25
        window_start = min(max(int(np.floor(position)) - 2, 0), coarse_count - 6)
        for tap_index in range(6):
            weight_value = 1.0
            for other_tap in range(6):
                if other_tap != tap_index:
                    weight_value *= (position - window_start - other_tap) / (tap_index - other_tap)
            table_rows[target, window_start + tap_index] = weight_value
    return table_rows


def local_phi_table(local_count):
    table_rows = np.zeros((2 * local_count, local_count + 2 * halo))
    for target in range(2 * local_count):
        if target % 2 == 0:
            table_rows[target, target // 2 + halo] = 1.0
        else:
            middle = (target - 1) // 2
            for offset in range(6):
                table_rows[target, middle + 1 + offset] = midpoint_taps[offset] / 256.0
    return table_rows


def spectra_kernel(chunks, parents, ranks, ways, plan, *refs):
    packed, refs = refs[:chunks], refs[chunks:]
    keeps, octants, signs, lasts, refs = *refs[:4], refs[4:]
    used = sum(len(pieces) for pieces in plan)
    flat_weights, refs = refs[:used], refs[used:]
    waves, table, choice, refs = *refs[:3], refs[3:]
    own_out, out, refs = refs[0], refs[1], refs[2:]
    columns, refs = refs[:chunks], refs[chunks:]
    running, staged, sent, held, ready, cosine, sine, operators, picked = refs[:9]
    dir_send, dir_recv, ghost_send, ghost_recv, keep_sem, box_send, box_recv, own_sem = refs[9:]
    weights = []
    for pieces in plan:
        weights.append(flat_weights[: len(pieces)])
        flat_weights = flat_weights[len(pieces) :]

    rows = held.shape[1] // chunks
    points = running.shape[1]
    width = held.shape[2]
    half = width // 2
    children = columns[0].shape[0]
    share = (children - straddle) // ways
    me = lax.axis_index("box")
    side = lax.axis_index("dir")

    def to_box(target):
        return dict(device_id={"box": target}, device_id_type=pl.DeviceIdType.MESH)

    def to_dir(target):
        return dict(device_id={"dir": target}, device_id_type=pl.DeviceIdType.MESH)

    barrier = pltpu.get_barrier_semaphore()
    for offset in range(1, ranks):
        pl.semaphore_signal(barrier, inc=1, **to_box(lax.rem(me + offset, ranks)))
    for offset in range(1, ways):
        pl.semaphore_signal(barrier, inc=1, **to_dir(lax.rem(side + offset, ways)))
    pl.semaphore_wait(barrier, ranks + ways - 2)

    def dir_copy(piece, offset):
        target = lax.rem(side + offset, ways)
        return pltpu.make_async_remote_copy(
            src_ref=packed[piece].at[target],
            dst_ref=columns[piece].at[pl.ds(straddle + side * share, share)],
            send_sem=dir_send.at[piece, offset - 1],
            recv_sem=dir_recv.at[piece, offset - 1],
            **to_dir(target),
        )

    def dir_kept(piece):
        source = packed[piece].at[side]
        landing = columns[piece].at[pl.ds(straddle + side * share, share)]
        return pltpu.make_async_copy(source, landing, keep_sem.at[piece])

    def ghost_copy(piece):
        source = columns[piece].at[pl.ds(children - straddle, straddle)]
        return pltpu.make_async_remote_copy(
            src_ref=source,
            dst_ref=columns[piece].at[pl.ds(0, straddle)],
            send_sem=ghost_send.at[piece],
            recv_sem=ghost_recv.at[piece],
            **to_box(me + 1),
        )

    def box_copy(phase, chunk, offset):
        target = lax.rem(me + offset, ranks)
        span = pl.ds(chunk * rows, rows)
        if phase == 0:
            source = sent.at[chunk, pl.ds(pl.multiple_of(target * rows, 16), rows)]
        else:
            source = ready.at[target, span]
        landing = held if phase == 0 else out
        return pltpu.make_async_remote_copy(
            src_ref=source,
            dst_ref=landing.at[me, span],
            send_sem=box_send.at[phase, chunk, offset - 1],
            recv_sem=box_recv.at[phase, chunk, offset - 1],
            **to_box(target),
        )

    def box_kept(phase, chunk):
        span = pl.ds(chunk * rows, rows)
        if phase == 0:
            source = sent.at[chunk, pl.ds(pl.multiple_of(me * rows, 16), rows)]
        else:
            source = ready.at[me, span]
        landing = held if phase == 0 else out
        return pltpu.make_async_copy(source, landing.at[me, span], own_sem.at[phase, chunk])

    def own_copy(chunk):
        return pltpu.make_async_copy(
            staged.at[chunk], own_out.at[:, pl.ds(chunk * points, points)], own_sem.at[2, chunk]
        )

    order = sorted(range(1, ranks), key=lambda offset: abs(offset - ranks / 2))

    def forward_ghosts(piece):
        @pl.when(me < ranks - 1)
        def _():
            ghost_copy(piece).start()

    def await_ghosts(piece):
        @pl.when(me > 0)
        def _():
            ghost_copy(piece).wait_recv()

    for piece in range(chunks):
        for offset in range(1, ways):
            dir_copy(piece, offset).start()
        dir_kept(piece).start()

    @pl.when(me == 0)
    def _():
        for piece in range(chunks):
            columns[piece][0:straddle] = jnp.zeros((straddle,) + columns[piece].shape[1:], jnp.bfloat16)

    running[0] = jnp.zeros(running.shape[1:], jnp.float32)
    strip = 32

    @pl.loop(0, chunks * points // strip)
    def _(index):
        span = pl.ds(pl.multiple_of(index * strip, strip), strip)
        along_x, along_y, along_z = waves[0, span], waves[1, span], waves[2, span]
        for octant in range(4):
            angle = along_z + along_x if octant % 2 else along_z - along_x
            angle = angle + along_y if octant // 2 else angle - along_y
            cosine[octant, span] = jnp.cos(angle)
            sine[octant, span] = jnp.sin(angle)

    everyone = choice.shape[0]
    entries = lax.broadcasted_iota(jnp.int32, (table.shape[2], everyone), 0)

    @pl.loop(0, everyone // 16)
    def _(batch):
        low = pl.multiple_of(batch * 16, 16)
        rows_of = choice[pl.ds(low, 16)]
        for member in range(16):
            chosen = (entries == rows_of[member : member + 1] - 1).astype(jnp.bfloat16)
            for part in range(2):
                picked[part, member] = jnp.dot(
                    table[part], chosen, preferred_element_type=jnp.float32
                )

        @pl.loop(0, table.shape[1] // 8)
        def _(tile):
            start = pl.multiple_of(tile * 8, 8)
            for part in range(2):
                block = jnp.swapaxes(picked[part, :, pl.ds(start, 8), :], 0, 1)
                operators[pl.ds(start, 8), pl.ds(part * everyone + low, 16), :] = block.astype(
                    jnp.bfloat16
                )

    for chunk in range(chunks):
        dir_kept(chunk).wait()
        for offset in range(1, ways):
            dir_copy(chunk, offset).wait_recv()
        forward_ghosts(chunk)
        await_ghosts(chunk)

        @pl.loop(0, children)
        def _(child):
            lifted = None
            for piece, weight in zip(plan[chunk], weights[chunk]):
                part = jnp.dot(
                    weight[...], columns[piece][child], preferred_element_type=jnp.float32
                )
                lifted = part if lifted is None else lifted + part
            octant = octants[child]
            keep = keeps[child]
            span = pl.ds(chunk * points, points)
            turn_cos = cosine[octant, span, :]
            turn_sin = sine[octant, span, :] * signs[child]
            real_part = lifted[:, :half]
            imag_part = lifted[:, half:]
            running[child + 1, :, :half] = (
                keep * running[child, :, :half] + turn_cos * real_part - turn_sin * imag_part
            )
            running[child + 1, :, half:] = (
                keep * running[child, :, half:] + turn_sin * real_part + turn_cos * imag_part
            )

        @pl.loop(0, points // 16)
        def _(tile):
            span = pl.ds(pl.multiple_of(tile * 16, 16), 16)
            values = [running[lasts[parent], span, :] for parent in range(parents)]
            for parent in range(parents):
                staged[chunk, parent, span] = values[parent].astype(jnp.bfloat16)
            for part in range(2):
                block = jnp.stack([value[8 * part : 8 * part + 8] for value in values])
                block = jnp.swapaxes(block, 0, 1).reshape(8 * parents, width)
                low = pl.multiple_of((2 * tile + part) * 8 * parents, 8 * parents)
                sent[chunk, pl.ds(low, 8 * parents)] = block.astype(jnp.bfloat16)

        for offset in order:
            box_copy(0, chunk, offset).start()
        box_kept(0, chunk).start()
        own_copy(chunk).start()

    for chunk in range(chunks):
        for offset in order:
            box_copy(0, chunk, offset).wait_recv()
        box_kept(0, chunk).wait()
        first_point = chunk * (rows // parents)

        @pl.loop(0, rows // (2 * parents))
        def _(pair):
            span = pl.ds(pl.multiple_of(chunk * rows + pair * 2 * parents, 16), 2 * parents)
            both = [held[rank, span].astype(jnp.float32) for rank in range(ranks)]
            results = []
            for member in range(2):
                low = member * parents
                spectra = jnp.concatenate([value[low : low + parents] for value in both], axis=0)
                spectra = spectra.astype(jnp.bfloat16)
                product = jnp.dot(
                    operators[first_point + 2 * pair + member], spectra, preferred_element_type=jnp.float32
                )
                count = product.shape[0] // 2
                direct, cross = product[:count], product[count:]
                results.append(
                    jnp.concatenate(
                        [
                            direct[:, :half] - cross[:, half:],
                            direct[:, half:] + cross[:, :half],
                        ],
                        axis=1,
                    )
                )
            for rank in range(ranks):
                low = rank * parents
                value = jnp.concatenate(
                    [result[low : low + parents] for result in results], axis=0
                )
                ready[rank, span] = value.astype(jnp.bfloat16)

        for offset in order:
            box_copy(1, chunk, offset).start()
        box_kept(1, chunk).start()

    for chunk in range(chunks):
        for offset in order:
            box_copy(1, chunk, offset).wait_recv()
        box_kept(1, chunk).wait()
        own_copy(chunk).wait()

        @pl.when(me < ranks - 1)
        def _():
            ghost_copy(chunk).wait_send()

        for offset in range(1, ways):
            dir_copy(chunk, offset).wait_send()
        for phase in range(2):
            for offset in order:
                box_copy(phase, chunk, offset).wait_send()


def spectra(packed, scalars, plan, weights, waves, table, choice, parents, ranks):
    chunks = len(plan)
    ways = packed[0].shape[0]
    children = ways * packed[0].shape[1] + straddle
    width = packed[0].shape[-1]
    points = weights[0][0].shape[0]
    rows = points * parents // ranks
    whole = (ranks, chunks * rows, width)
    arrays = [*packed, *scalars, *sum(weights, []), waves, table, choice]
    in_specs = [pl.BlockSpec(memory_space=pl.ANY)] * chunks
    in_specs += [pl.BlockSpec(memory_space=pltpu.SMEM)] * len(scalars)
    in_specs += [pl.BlockSpec(memory_space=pltpu.VMEM)] * (len(arrays) - len(in_specs))
    piece_rows = [piece.shape[2] for piece in packed]
    everyone = choice.shape[0]
    turns = pltpu.VMEM((4,) + waves.shape[1:], jnp.float32)
    dma = pltpu.SemaphoreType.DMA
    return pl.pallas_call(
        functools.partial(spectra_kernel, chunks, parents, ranks, ways, plan),
        in_specs=in_specs,
        out_specs=[pl.BlockSpec(memory_space=pl.ANY)] * 2,
        out_shape=[
            jax.ShapeDtypeStruct((parents, chunks * points, width), jnp.bfloat16),
            jax.ShapeDtypeStruct(whole, jnp.bfloat16),
        ],
        scratch_shapes=[
            *[pltpu.VMEM((children, count, width), jnp.bfloat16) for count in piece_rows],
            pltpu.VMEM((children + 1, points, width), jnp.float32),
            pltpu.VMEM((chunks, parents, points, width), jnp.bfloat16),
            pltpu.VMEM((chunks, ranks * rows, width), jnp.bfloat16),
            pltpu.VMEM(whole, jnp.bfloat16),
            pltpu.VMEM(whole, jnp.bfloat16),
            turns,
            turns,
            pltpu.VMEM((table.shape[1], 2 * everyone, everyone), jnp.bfloat16),
            pltpu.VMEM((2, 16, table.shape[1], everyone), jnp.float32),
            dma((chunks, ways - 1)),
            dma((chunks, ways - 1)),
            dma((chunks,)),
            dma((chunks,)),
            dma((chunks,)),
            dma((2, chunks, ranks - 1)),
            dma((2, chunks, ranks - 1)),
            dma((3, chunks)),
        ],
        compiler_params=pltpu.CompilerParams(
            collective_id=0, has_side_effects=True, vmem_limit_bytes=58 * 2**20
        ),
        name="spectra",
    )(*arrays)


def shared_out(block, ways):
    local_count = block.shape[2] // ways
    ring = jnp.concatenate([block[:, :, -halo:], block, block[:, :, :halo]], axis=2)
    width = local_count + 2 * halo
    parts = [ring[:, :, way * local_count : way * local_count + width] for way in range(ways)]
    stacked = jnp.stack(parts)
    stacked = stacked.reshape(ways, block.shape[0], block.shape[1] * width, block.shape[3])
    spare = -stacked.shape[2] % 16
    return jnp.pad(stacked, ((0, 0), (0, 0), (0, spare), (0, 0)))


def chunk_plan(coarse_count, chunks):
    table = theta_table(coarse_count)
    fine_chunk = 2 * coarse_count // chunks
    needed = []
    for chunk in range(chunks):
        used = np.nonzero(table[chunk * fine_chunk : (chunk + 1) * fine_chunk].any(axis=0))[0]
        needed.append((int(used[0]), int(used[-1]) + 1))
    starts = [0] + [end for _, end in needed[:-1]]
    return [(start, end) for start, (_, end) in zip(starts, needed)], needed


def local(child_spectra, child_ids, translators, trans_index):
    ways = lax.axis_size("dir")
    rows = lax.axis_size("box")
    theta_coarse, phi_coarse, width = child_spectra.shape[1:]
    row_children = child_ids.shape[0]
    theta_fine = 2 * theta_coarse
    local_coarse = phi_coarse // ways
    local_fine = 2 * local_coarse
    parents_all = trans_index.shape[0]
    parents = parents_all // rows
    chunks = next(count for count in (3, 2, 1) if theta_fine % (count * rows) == 0)
    fine_chunk = theta_fine // chunks
    theta_local = fine_chunk // rows
    points = theta_local * local_fine
    box_rank = lax.axis_index("box")
    dir_rank = lax.axis_index("dir")
    segments, needed = chunk_plan(theta_coarse, chunks)

    forward = [(source, source + 1) for source in range(rows - 1)]
    ghost_ids = lax.ppermute(child_ids[-straddle:], "box", forward)
    ghost_ids = jnp.where(box_rank > 0, ghost_ids, -8)
    all_ids = jnp.concatenate([ghost_ids, child_ids])
    slots = all_ids // 8 - box_rank * parents
    octants = all_ids % 8
    same = slots[1:] == slots[:-1]
    keeps = jnp.concatenate([jnp.zeros((1,), jnp.float32), same.astype(jnp.float32)])
    upper = octants >= 4
    signs = jnp.where(upper, 1.0, -1.0).astype(jnp.float32)
    mirrored = jnp.where(upper, octants - 4, 3 - octants)
    slot_range = jnp.arange(parents, dtype=jnp.int32)
    lasts = jnp.sum((slots[None, :] <= slot_range[:, None]).astype(jnp.int32), axis=1)

    packed = [shared_out(child_spectra[:, start:end], ways) for start, end in segments]

    place = (theta_fine, local_fine, width // 2)
    theta_index = lax.broadcasted_iota(jnp.int32, place, 0).astype(jnp.float32)
    phi_index = lax.broadcasted_iota(jnp.int32, place, 1) + dir_rank * local_fine
    theta_angles = jnp.pi * (theta_index + 0.5) / theta_fine
    phi_angles = 2.0 * jnp.pi * phi_index.astype(jnp.float32) / (local_fine * ways)
    sine_theta = wave_shift * jnp.sin(theta_angles)
    waves = jnp.stack(
        [
            sine_theta * jnp.cos(phi_angles),
            sine_theta * jnp.sin(phi_angles),
            wave_shift * jnp.cos(theta_angles),
        ]
    ).reshape(3, theta_fine * local_fine, width // 2)

    theta_weights = theta_table(theta_coarse).astype(ml_dtypes.bfloat16).astype(np.float64)
    phi_weights = local_phi_table(local_coarse)

    count = translators.shape[1]
    split = translators.reshape(2, count, chunks, rows, theta_local, local_fine)
    own = lax.dynamic_index_in_dim(split, box_rank, 3, keepdims=False)
    own = own.reshape(2, count, chunks * points).transpose(0, 2, 1)
    table = jnp.pad(own, ((0, 0), (0, -own.shape[1] % 8), (0, -count % 64)))
    own_shape = (parents, theta_fine, local_fine, width)

    plan, weights = [], []
    for chunk in range(chunks):
        low, high = needed[chunk]
        used = [
            index for index, (start, end) in enumerate(segments) if start < high and end > low
        ]
        tables = []
        for index in used:
            start, end = segments[index]
            product = np.einsum(
                "ht,gj->hgtj",
                theta_weights[chunk * fine_chunk : (chunk + 1) * fine_chunk, start:end],
                phi_weights,
            )
            product = product.reshape(fine_chunk * local_fine, -1)
            product = np.pad(product, ((0, 0), (0, -product.shape[1] % 16)))
            tables.append(jnp.asarray(product.astype(ml_dtypes.bfloat16)))
        plan.append(used)
        weights.append(tables)
    parent_spectra, incoming = spectra(
        packed,
        (keeps, mirrored, signs, lasts),
        plan,
        weights,
        waves,
        table,
        trans_index,
        parents,
        rows,
    )
    incoming = incoming.reshape(rows, chunks, theta_local, local_fine, parents, width)
    incoming = incoming.transpose(4, 1, 0, 2, 3, 5).reshape(own_shape)
    return parent_spectra.reshape(own_shape), incoming


def solution(mesh):
    return jax.shard_map(
        local,
        mesh=mesh,
        in_specs=(P(("box", "dir"), None, None, None), P("box"), P(None, None, None, "dir"), P()),
        out_specs=(P("box", None, "dir", None), P("box", None, "dir", None)),
        check_vma=False,
    )
```

```python
import functools

import jax
import jax.numpy as jnp
import ml_dtypes
import numpy as np
from jax import lax
from jax.experimental import pallas as pl
from jax.experimental.pallas import tpu as pltpu
from jax.sharding import PartitionSpec as P

wave_shift = 5.0
midpoint_taps = (3.0, -25.0, 150.0, 150.0, -25.0, 3.0)
halo = 3
straddle = 3


def theta_table(coarse_count):
    fine_count = 2 * coarse_count
    table_rows = np.zeros((fine_count, coarse_count))
    for target in range(fine_count):
        position = target / 2.0 - 0.25
        window_start = min(max(int(np.floor(position)) - 2, 0), coarse_count - 6)
        for tap_index in range(6):
            weight_value = 1.0
            for other_tap in range(6):
                if other_tap != tap_index:
                    weight_value *= (position - window_start - other_tap) / (tap_index - other_tap)
            table_rows[target, window_start + tap_index] = weight_value
    return table_rows


def local_phi_table(local_count):
    table_rows = np.zeros((2 * local_count, local_count + 2 * halo))
    for target in range(2 * local_count):
        if target % 2 == 0:
            table_rows[target, target // 2 + halo] = 1.0
        else:
            middle = (target - 1) // 2
            for offset in range(6):
                table_rows[target, middle + 1 + offset] = midpoint_taps[offset] / 256.0
    return table_rows


def spectra_kernel(chunks, parents, ranks, ways, plan, bounds, *refs):
    packed, refs = refs[0], refs[1:]
    keeps, octants, signs, lasts, refs = *refs[:4], refs[4:]
    used = sum(len(pieces) for pieces in plan)
    flat_weights, refs = refs[:used], refs[used:]
    waves, table, choice, refs = *refs[:3], refs[3:]
    own_out, out, refs = refs[0], refs[1], refs[2:]
    columns, refs = refs[:chunks], refs[chunks:]
    running, staged, sent, held, ready, cosine, sine, operators, picked = refs[:9]
    dir_send, dir_recv, ghost_send, ghost_recv, keep_sem, box_send, box_recv, own_sem = refs[9:]
    weights = []
    for pieces in plan:
        weights.append(flat_weights[: len(pieces)])
        flat_weights = flat_weights[len(pieces) :]

    rows = held.shape[1] // chunks
    points = running.shape[1]
    width = held.shape[2]
    half = width // 2
    children = columns[0].shape[0]
    share = (children - straddle) // ways
    me = lax.axis_index("box")
    side = lax.axis_index("dir")

    def to_box(target):
        return dict(device_id={"box": target}, device_id_type=pl.DeviceIdType.MESH)

    def to_dir(target):
        return dict(device_id={"dir": target}, device_id_type=pl.DeviceIdType.MESH)

    barrier = pltpu.get_barrier_semaphore()
    for offset in range(1, ranks):
        pl.semaphore_signal(barrier, inc=1, **to_box(lax.rem(me + offset, ranks)))
    for offset in range(1, ways):
        pl.semaphore_signal(barrier, inc=1, **to_dir(lax.rem(side + offset, ways)))
    pl.semaphore_wait(barrier, ranks + ways - 2)

    def dir_copy(piece, offset):
        target = lax.rem(side + offset, ways)
        return pltpu.make_async_remote_copy(
            src_ref=packed.at[target, :, pl.ds(bounds[piece], bounds[piece + 1] - bounds[piece])],
            dst_ref=columns[piece].at[pl.ds(straddle + side * share, share)],
            send_sem=dir_send.at[piece, offset - 1],
            recv_sem=dir_recv.at[piece, offset - 1],
            **to_dir(target),
        )

    def dir_kept(piece):
        source = packed.at[side, :, pl.ds(bounds[piece], bounds[piece + 1] - bounds[piece])]
        landing = columns[piece].at[pl.ds(straddle + side * share, share)]
        return pltpu.make_async_copy(source, landing, keep_sem.at[piece])

    def ghost_copy(piece):
        source = columns[piece].at[pl.ds(children - straddle, straddle)]
        return pltpu.make_async_remote_copy(
            src_ref=source,
            dst_ref=columns[piece].at[pl.ds(0, straddle)],
            send_sem=ghost_send.at[piece],
            recv_sem=ghost_recv.at[piece],
            **to_box(me + 1),
        )

    def box_copy(phase, chunk, offset):
        target = lax.rem(me + offset, ranks)
        span = pl.ds(chunk * rows, rows)
        if phase == 0:
            source = sent.at[chunk, pl.ds(pl.multiple_of(target * rows, 16), rows)]
        else:
            source = ready.at[target, span]
        landing = held if phase == 0 else out
        return pltpu.make_async_remote_copy(
            src_ref=source,
            dst_ref=landing.at[me, span],
            send_sem=box_send.at[phase, chunk, offset - 1],
            recv_sem=box_recv.at[phase, chunk, offset - 1],
            **to_box(target),
        )

    def box_kept(phase, chunk):
        span = pl.ds(chunk * rows, rows)
        if phase == 0:
            source = sent.at[chunk, pl.ds(pl.multiple_of(me * rows, 16), rows)]
        else:
            source = ready.at[me, span]
        landing = held if phase == 0 else out
        return pltpu.make_async_copy(source, landing.at[me, span], own_sem.at[phase, chunk])

    def own_copy(chunk):
        return pltpu.make_async_copy(
            staged.at[chunk], own_out.at[:, pl.ds(chunk * points, points)], own_sem.at[2, chunk]
        )

    order = sorted(range(1, ranks), key=lambda offset: abs(offset - ranks / 2))

    def forward_ghosts(piece):
        @pl.when(me < ranks - 1)
        def _():
            ghost_copy(piece).start()

    def await_ghosts(piece):
        @pl.when(me > 0)
        def _():
            ghost_copy(piece).wait_recv()

    for piece in range(chunks):
        for offset in range(1, ways):
            dir_copy(piece, offset).start()
        dir_kept(piece).start()

    @pl.when(me == 0)
    def _():
        for piece in range(chunks):
            columns[piece][0:straddle] = jnp.zeros((straddle,) + columns[piece].shape[1:], jnp.bfloat16)

    running[0] = jnp.zeros(running.shape[1:], jnp.float32)
    strip = 32

    @pl.loop(0, chunks * points // strip)
    def _(index):
        span = pl.ds(pl.multiple_of(index * strip, strip), strip)
        along_x, along_y, along_z = waves[0, span], waves[1, span], waves[2, span]
        for octant in range(4):
            angle = along_z + along_x if octant % 2 else along_z - along_x
            angle = angle + along_y if octant // 2 else angle - along_y
            cosine[octant, span] = jnp.cos(angle)
            sine[octant, span] = jnp.sin(angle)

    everyone = choice.shape[0]
    entries = lax.broadcasted_iota(jnp.int32, (table.shape[2], everyone), 0)

    @pl.loop(0, everyone // 16)
    def _(batch):
        low = pl.multiple_of(batch * 16, 16)
        rows_of = choice[pl.ds(low, 16)]
        for member in range(16):
            chosen = (entries == rows_of[member : member + 1] - 1).astype(jnp.bfloat16)
            for part in range(2):
                picked[part, member] = jnp.dot(
                    table[part], chosen, preferred_element_type=jnp.float32
                )

        @pl.loop(0, table.shape[1] // 8)
        def _(tile):
            start = pl.multiple_of(tile * 8, 8)
            for part in range(2):
                block = jnp.swapaxes(picked[part, :, pl.ds(start, 8), :], 0, 1)
                operators[pl.ds(start, 8), pl.ds(part * everyone + low, 16), :] = block.astype(
                    jnp.bfloat16
                )

    for chunk in range(chunks):
        dir_kept(chunk).wait()
        for offset in range(1, ways):
            dir_copy(chunk, offset).wait_recv()
        forward_ghosts(chunk)
        await_ghosts(chunk)

        @pl.loop(0, children)
        def _(child):
            lifted = None
            for piece, weight in zip(plan[chunk], weights[chunk]):
                part = jnp.dot(
                    weight[...], columns[piece][child], preferred_element_type=jnp.float32
                )
                lifted = part if lifted is None else lifted + part
            octant = octants[child]
            keep = keeps[child]
            span = pl.ds(chunk * points, points)
            turn_cos = cosine[octant, span, :]
            turn_sin = sine[octant, span, :] * signs[child]
            real_part = lifted[:, :half]
            imag_part = lifted[:, half:]
            running[child + 1, :, :half] = (
                keep * running[child, :, :half] + turn_cos * real_part - turn_sin * imag_part
            )
            running[child + 1, :, half:] = (
                keep * running[child, :, half:] + turn_sin * real_part + turn_cos * imag_part
            )

        @pl.loop(0, points // 16)
        def _(tile):
            span = pl.ds(pl.multiple_of(tile * 16, 16), 16)
            values = [running[lasts[parent], span, :] for parent in range(parents)]
            for parent in range(parents):
                staged[chunk, parent, span] = values[parent].astype(jnp.bfloat16)
            for part in range(2):
                block = jnp.stack([value[8 * part : 8 * part + 8] for value in values])
                block = jnp.swapaxes(block, 0, 1).reshape(8 * parents, width)
                low = pl.multiple_of((2 * tile + part) * 8 * parents, 8 * parents)
                sent[chunk, pl.ds(low, 8 * parents)] = block.astype(jnp.bfloat16)

        for offset in order:
            box_copy(0, chunk, offset).start()
        box_kept(0, chunk).start()
        own_copy(chunk).start()

    for chunk in range(chunks):
        for offset in order:
            box_copy(0, chunk, offset).wait_recv()
        box_kept(0, chunk).wait()
        first_point = chunk * (rows // parents)

        @pl.loop(0, rows // (2 * parents))
        def _(pair):
            span = pl.ds(pl.multiple_of(chunk * rows + pair * 2 * parents, 16), 2 * parents)
            both = [held[rank, span].astype(jnp.float32) for rank in range(ranks)]
            results = []
            for member in range(2):
                low = member * parents
                spectra = jnp.concatenate([value[low : low + parents] for value in both], axis=0)
                spectra = spectra.astype(jnp.bfloat16)
                product = jnp.dot(
                    operators[first_point + 2 * pair + member], spectra, preferred_element_type=jnp.float32
                )
                count = product.shape[0] // 2
                direct, cross = product[:count], product[count:]
                results.append(
                    jnp.concatenate(
                        [
                            direct[:, :half] - cross[:, half:],
                            direct[:, half:] + cross[:, :half],
                        ],
                        axis=1,
                    )
                )
            for rank in range(ranks):
                low = rank * parents
                value = jnp.concatenate(
                    [result[low : low + parents] for result in results], axis=0
                )
                ready[rank, span] = value.astype(jnp.bfloat16)

        for offset in order:
            box_copy(1, chunk, offset).start()
        box_kept(1, chunk).start()

    for chunk in range(chunks):
        for offset in order:
            box_copy(1, chunk, offset).wait_recv()
        box_kept(1, chunk).wait()
        own_copy(chunk).wait()

        @pl.when(me < ranks - 1)
        def _():
            ghost_copy(chunk).wait_send()

        for offset in range(1, ways):
            dir_copy(chunk, offset).wait_send()
        for phase in range(2):
            for offset in order:
                box_copy(phase, chunk, offset).wait_send()


def spectra(packed, scalars, plan, bounds, weights, waves, table, choice, parents, ranks):
    chunks = len(plan)
    ways = packed.shape[0]
    children = ways * packed.shape[1] + straddle
    width = packed.shape[-1]
    points = weights[0][0].shape[0]
    rows = points * parents // ranks
    whole = (ranks, chunks * rows, width)
    arrays = [packed, *scalars, *sum(weights, []), waves, table, choice]
    in_specs = [pl.BlockSpec(memory_space=pl.ANY)]
    in_specs += [pl.BlockSpec(memory_space=pltpu.SMEM)] * len(scalars)
    in_specs += [pl.BlockSpec(memory_space=pltpu.VMEM)] * (len(arrays) - len(in_specs))
    piece_rows = [high - low for low, high in zip(bounds, bounds[1:])]
    everyone = choice.shape[0]
    turns = pltpu.VMEM((4,) + waves.shape[1:], jnp.float32)
    dma = pltpu.SemaphoreType.DMA
    return pl.pallas_call(
        functools.partial(spectra_kernel, chunks, parents, ranks, ways, plan, bounds),
        in_specs=in_specs,
        out_specs=[pl.BlockSpec(memory_space=pl.ANY)] * 2,
        out_shape=[
            jax.ShapeDtypeStruct((parents, chunks * points, width), jnp.bfloat16),
            jax.ShapeDtypeStruct(whole, jnp.bfloat16),
        ],
        scratch_shapes=[
            *[pltpu.VMEM((children, count, width), jnp.bfloat16) for count in piece_rows],
            pltpu.VMEM((children + 1, points, width), jnp.float32),
            pltpu.VMEM((chunks, parents, points, width), jnp.bfloat16),
            pltpu.VMEM((chunks, ranks * rows, width), jnp.bfloat16),
            pltpu.VMEM(whole, jnp.bfloat16),
            pltpu.VMEM(whole, jnp.bfloat16),
            turns,
            turns,
            pltpu.VMEM((table.shape[1], 2 * everyone, everyone), jnp.bfloat16),
            pltpu.VMEM((2, 16, table.shape[1], everyone), jnp.float32),
            dma((chunks, ways - 1)),
            dma((chunks, ways - 1)),
            dma((chunks,)),
            dma((chunks,)),
            dma((chunks,)),
            dma((2, chunks, ranks - 1)),
            dma((2, chunks, ranks - 1)),
            dma((3, chunks)),
        ],
        compiler_params=pltpu.CompilerParams(
            collective_id=0, has_side_effects=True, vmem_limit_bytes=58 * 2**20
        ),
        name="spectra",
    )(*arrays)


def shared_out(block, ways):
    local_count = block.shape[2] // ways
    ring = jnp.concatenate([block[:, :, -halo:], block, block[:, :, :halo]], axis=2)
    width = local_count + 2 * halo
    parts = [ring[:, :, way * local_count : way * local_count + width] for way in range(ways)]
    stacked = jnp.stack(parts)
    stacked = stacked.reshape(ways, block.shape[0], block.shape[1] * width, block.shape[3])
    spare = -stacked.shape[2] % 16
    return jnp.pad(stacked, ((0, 0), (0, 0), (0, spare), (0, 0)))


def chunk_plan(coarse_count, chunks):
    table = theta_table(coarse_count)
    fine_chunk = 2 * coarse_count // chunks
    needed = []
    for chunk in range(chunks):
        used = np.nonzero(table[chunk * fine_chunk : (chunk + 1) * fine_chunk].any(axis=0))[0]
        needed.append((int(used[0]), int(used[-1]) + 1))
    return needed


def local(child_spectra, child_ids, translators, trans_index):
    ways = lax.axis_size("dir")
    rows = lax.axis_size("box")
    theta_coarse, phi_coarse, width = child_spectra.shape[1:]
    row_children = child_ids.shape[0]
    theta_fine = 2 * theta_coarse
    local_coarse = phi_coarse // ways
    local_fine = 2 * local_coarse
    parents_all = trans_index.shape[0]
    parents = parents_all // rows
    chunks = next(count for count in (3, 2, 1) if theta_fine % (count * rows) == 0)
    fine_chunk = theta_fine // chunks
    theta_local = fine_chunk // rows
    points = theta_local * local_fine
    box_rank = lax.axis_index("box")
    dir_rank = lax.axis_index("dir")
    needed = chunk_plan(theta_coarse, chunks)

    forward = [(source, source + 1) for source in range(rows - 1)]
    ghost_ids = lax.ppermute(child_ids[-straddle:], "box", forward)
    ghost_ids = jnp.where(box_rank > 0, ghost_ids, -8)
    all_ids = jnp.concatenate([ghost_ids, child_ids])
    slots = all_ids // 8 - box_rank * parents
    octants = all_ids % 8
    same = slots[1:] == slots[:-1]
    keeps = jnp.concatenate([jnp.zeros((1,), jnp.float32), same.astype(jnp.float32)])
    upper = octants >= 4
    signs = jnp.where(upper, 1.0, -1.0).astype(jnp.float32)
    mirrored = jnp.where(upper, octants - 4, 3 - octants)
    slot_range = jnp.arange(parents, dtype=jnp.int32)
    lasts = jnp.sum((slots[None, :] <= slot_range[:, None]).astype(jnp.int32), axis=1)

    packed = shared_out(child_spectra, ways)
    taps = local_coarse + 2 * halo
    bounds = [0] + [-(-end * taps // 16) * 16 for _, end in needed[:-1]] + [packed.shape[2]]

    place = (theta_fine, local_fine, width // 2)
    theta_index = lax.broadcasted_iota(jnp.int32, place, 0).astype(jnp.float32)
    phi_index = lax.broadcasted_iota(jnp.int32, place, 1) + dir_rank * local_fine
    theta_angles = jnp.pi * (theta_index + 0.5) / theta_fine
    phi_angles = 2.0 * jnp.pi * phi_index.astype(jnp.float32) / (local_fine * ways)
    sine_theta = wave_shift * jnp.sin(theta_angles)
    waves = jnp.stack(
        [
            sine_theta * jnp.cos(phi_angles),
            sine_theta * jnp.sin(phi_angles),
            wave_shift * jnp.cos(theta_angles),
        ]
    ).reshape(3, theta_fine * local_fine, width // 2)

    theta_weights = theta_table(theta_coarse).astype(ml_dtypes.bfloat16).astype(np.float64)
    phi_weights = local_phi_table(local_coarse)

    count = translators.shape[1]
    split = translators.reshape(2, count, chunks, rows, theta_local, local_fine)
    own = lax.dynamic_index_in_dim(split, box_rank, 3, keepdims=False)
    own = own.reshape(2, count, chunks * points).transpose(0, 2, 1)
    table = jnp.pad(own, ((0, 0), (0, -own.shape[1] % 8), (0, -count % 64)))
    own_shape = (parents, theta_fine, local_fine, width)

    plan, weights = [], []
    for chunk in range(chunks):
        low, high = needed[chunk]
        product = np.einsum(
            "ht,gj->hgtj",
            theta_weights[chunk * fine_chunk : (chunk + 1) * fine_chunk],
            phi_weights,
        )
        product = product.reshape(fine_chunk * local_fine, -1)
        product = np.pad(product, ((0, 0), (0, bounds[-1] - product.shape[1])))
        product = product.astype(ml_dtypes.bfloat16)
        used = [
            index
            for index in range(chunks)
            if bounds[index] < high * taps and bounds[index + 1] > low * taps
        ]
        tables = [jnp.asarray(product[:, bounds[index] : bounds[index + 1]]) for index in used]
        plan.append(used)
        weights.append(tables)
    parent_spectra, incoming = spectra(
        packed,
        (keeps, mirrored, signs, lasts),
        plan,
        bounds,
        weights,
        waves,
        table,
        trans_index,
        parents,
        rows,
    )
    incoming = incoming.reshape(rows, chunks, theta_local, local_fine, parents, width)
    incoming = incoming.transpose(4, 1, 0, 2, 3, 5).reshape(own_shape)
    return parent_spectra.reshape(own_shape), incoming


def solution(mesh):
    return jax.shard_map(
        local,
        mesh=mesh,
        in_specs=(P(("box", "dir"), None, None, None), P("box"), P(None, None, None, "dir"), P()),
        out_specs=(P("box", None, "dir", None), P("box", None, "dir", None)),
        check_vma=False,
    )
```
